32 devices in a mesh: ind: 16 (over z, y, core), slab: 2 (over x).
Axes of the slice: x: 2, y: 2, z: 4, core: 2. Of those that a mesh axis runs over, the one named last changes fastest.
Arguments:
- dosages: float32 [8192, 2048], P('ind', 'slab'), may hold values from 0 to 2
- tile_rows: int32 [256], P('ind'), may hold values from -1 to 15, as said below
- tile_cols: int32 [256], P('ind'), may hold values from -1 to 15, as said below
Outputs:
- allele_freq: float32 [2048], P('slab')
- grm_tiles: float32 [256, 512, 512], P(('ind', 'slab'))
The draws below stay inside these ranges and needn't reach their ends.
Inputs may be any that keep to these rules, and one draw needn't show every extreme that they name: `tile_rows`: slots s * 16 to (s + 1) * 16 - 1 belong to owner s. An owner's listed tiles fill its first slots and the rest are -1; every owner lists 2 or more tiles, and some owner fills all 16 slots in every draw. `tile_cols`: -1 exactly where tile_rows is -1; elsewhere not below tile_rows at the same slot.
All inputs are finite; a program needn't handle non-finite values.
Results may differ from the reference program's by a relative error of at most 0.0011.
Values may be sent and summed in bfloat16 or wider, within the bound.
A program may use at most 128 MiB of HBM per device.

```python
import jax
import jax.numpy as jnp
from jax import lax

BLOCK = 512
VARIANTS = 2048
CAP = 16
INDIVIDUALS = 8192
N_IND = 16


def draw_dosages(key, part):
    key_base, key_first, key_second, key_blur, key_fuzz_one, key_fuzz_two = jax.random.split(key, 6)
    base_rate = jax.random.uniform(key_base, (VARIANTS,), jnp.float32, 0.0025, 0.3)
    log_blur = jax.random.uniform(key_blur, (VARIANTS,), jnp.float32, jnp.log(0.001), jnp.log(0.2))
    blur = jnp.exp(log_blur)
    row_place = jnp.arange(INDIVIDUALS, dtype=jnp.float32)
    chance = base_rate[None, :] * (1.0 + 2.0 * row_place[:, None] / INDIVIDUALS)
    first_allele = jax.random.uniform(key_first, (INDIVIDUALS, VARIANTS), jnp.float32) < chance
    second_allele = jax.random.uniform(key_second, (INDIVIDUALS, VARIANTS), jnp.float32) < chance
    fuzz_one = jax.random.uniform(key_fuzz_one, (INDIVIDUALS, VARIANTS), jnp.float32) * blur[None, :]
    fuzz_two = jax.random.uniform(key_fuzz_two, (INDIVIDUALS, VARIANTS), jnp.float32) * blur[None, :]
    first_value = jnp.where(first_allele, 1.0 - fuzz_one, fuzz_one)
    second_value = jnp.where(second_allele, 1.0 - fuzz_two, fuzz_two)
    return (first_value + second_value).astype(jnp.float32)


def tile_lists(key):
    key_count, key_full, key_first, key_second = jax.random.split(key, 4)
    listed_count = jax.random.randint(key_count, (N_IND,), CAP // 4, CAP + 1)
    full_owners = jax.random.permutation(key_full, N_IND)[:3]
    listed_count = listed_count.at[full_owners].set(CAP)
    first_block = jax.random.randint(key_first, (N_IND, CAP), 0, N_IND)
    second_block = jax.random.randint(key_second, (N_IND, CAP), 0, N_IND)
    lower_block = jnp.minimum(first_block, second_block)
    upper_block = jnp.maximum(first_block, second_block)
    used_slot = jnp.arange(CAP, dtype=jnp.int32)[None, :] < listed_count[:, None]
    row_list = jnp.where(used_slot, lower_block, -1).reshape(-1).astype(jnp.int32)
    col_list = jnp.where(used_slot, upper_block, -1).reshape(-1).astype(jnp.int32)
    return (row_list, col_list)


def draw_tile_rows(key, part):
    return tile_lists(jax.random.fold_in(key, 7))[0]


def draw_tile_cols(key, part):
    return tile_lists(jax.random.fold_in(key, 7))[1]


def setup_inputs(seed: int = 0) -> dict:
    splits = jax.random.split(jax.random.key(seed), 4)
    return {
        "dosages": draw_dosages(jax.random.fold_in(splits[3], 71), 0),
        "tile_rows": draw_tile_rows(jax.random.fold_in(splits[3], 71), 0),
        "tile_cols": draw_tile_cols(jax.random.fold_in(splits[3], 71), 0),
    }


def reference(dosages, tile_rows, tile_cols):
    counted = dosages.astype(jnp.float32)
    allele_freq = lax.optimization_barrier(jnp.sum(counted, axis=0)) / (2.0 * INDIVIDUALS)
    spread = jnp.maximum(2.0 * allele_freq * (1.0 - allele_freq), 0.05)
    standard = ((counted - 2.0 * allele_freq) * lax.rsqrt(spread)).astype(jnp.bfloat16)
    groups = standard.reshape(N_IND, BLOCK, VARIANTS)

    def one_tile(slot_index):
        row_block = tile_rows[slot_index]
        col_block = tile_cols[slot_index]
        left_part = groups[jnp.maximum(row_block, 0)].astype(jnp.float32)
        right_part = groups[jnp.maximum(col_block, 0)].astype(jnp.float32)
        product = jnp.dot(left_part, right_part.T, precision=lax.Precision.HIGHEST, preferred_element_type=jnp.float32)
        return jnp.where(row_block >= 0, product / VARIANTS, jnp.float32(0.0))
    grm_tiles = lax.map(one_tile, jnp.arange(N_IND * CAP, dtype=jnp.int32))
    return (allele_freq, grm_tiles)
```

```python
import functools

import jax
import jax.numpy as jnp
from jax import lax
from jax.experimental import pallas as pl
from jax.experimental.pallas import tpu as pltpu
from jax.sharding import PartitionSpec as P

MESH = pl.DeviceIdType.MESH
PIECES = 4
AHEAD = 4


def frequencies(total, people):
    allele_freq = total / (2.0 * people)
    spread = jnp.maximum(2.0 * allele_freq * (1.0 - allele_freq), 0.05)
    return allele_freq, spread


def gather_kernel(
    n, dosages_ref, freq_ref, blocks_ref,
    sums, own, sum_send, sum_recv, local_sem,
    x_send, y_send, up_send, down_send, core_send, column_recv, x_recv, y_recv, diag_recv, core_recv,
):
    rows, variants = own.shape
    zs = n // 4
    piece_rows = rows // PIECES
    me, x = lax.axis_index("ind"), lax.axis_index("slab")
    core, y, z = lax.rem(me, 2), lax.rem(me // 2, 2), me // 4

    def ind_of(z_, y_, core_):
        return (z_ * 2 + y_) * 2 + core_

    to_x = (me, 1 - x)
    to_y = (ind_of(z, 1 - y, core), x)
    to_core = (ind_of(z, y, 1 - core), x)
    to_up = (ind_of(jnp.minimum(z + 1, zs - 1), y, core), x)
    to_down = (ind_of(jnp.maximum(z - 1, 0), y, core), x)

    barrier = pltpu.get_barrier_semaphore()
    pl.semaphore_signal(barrier, inc=1, device_id=to_x, device_id_type=MESH)

    @pl.loop(1, n)
    def _(k):
        other = lax.rem(me + k, n)
        pl.semaphore_signal(barrier, inc=1, device_id=(other, x), device_id_type=MESH)

    sums[pl.ds(me, 1)] = jnp.sum(dosages_ref[...], axis=0).reshape(1, 1, variants)
    pl.semaphore_wait(barrier, n)

    def sum_copy(k, slot):
        other = lax.rem(me + k, n)
        return pltpu.make_async_remote_copy(
            src_ref=sums.at[slot], dst_ref=sums.at[slot],
            send_sem=sum_send.at[k], recv_sem=sum_recv.at[slot],
            device_id=(other, x), device_id_type=MESH,
        )

    @pl.loop(1, n)
    def _(k):
        sum_copy(k, me).start()

    @pl.loop(1, n)
    def _(k):
        sum_copy(k, lax.rem(me + k, n)).wait_recv()

    allele_freq, spread = frequencies(jnp.sum(sums[...], axis=0), rows * n)
    freq_ref[...] = allele_freq
    own[...] = ((dosages_ref[...] - 2.0 * allele_freq) * lax.rsqrt(spread)).astype(jnp.bfloat16)
    keep = pltpu.make_async_copy(own, blocks_ref.at[core, x, z * 2 + y], local_sem)
    keep.start()
    keep.wait()

    @pl.loop(1, n)
    def _(k):
        sum_copy(k, me).wait_send()

    def copy(x_, y_, z_, p, send_sem, recv_sem, to):
        part = blocks_ref.at[core, x_, z_ * 2 + y_, pl.ds(pl.multiple_of(p * piece_rows, piece_rows), piece_rows)]
        return pltpu.make_async_remote_copy(
            src_ref=part, dst_ref=part, send_sem=send_sem, recv_sem=recv_sem,
            device_id=to, device_id_type=MESH,
        )

    def hand_on(x_, y_, z_, p):
        copy(x_, y_, z_, p, core_send, core_recv, to_core).start()

    def nearest(step):
        near = jnp.minimum(z, zs - 1 - z)
        hop = (step + 1) // 2
        close = jnp.where(lax.rem(step, 2) == 1, z - hop, z + hop)
        far = jnp.where(z <= zs - 1 - z, step, zs - 1 - step)
        return jnp.where(step <= 2 * near, close, far)

    def from_column(i):
        z_, p = nearest(i // PIECES), lax.rem(i, PIECES)

        @pl.when(z_ != z)
        def _():
            copy(x, y, z_, p, x_send, column_recv.at[z_, p], to_x).wait_recv()

        @pl.when((z_ <= z) & (z < zs - 1))
        def _():
            copy(x, y, z_, p, up_send, column_recv.at[z_, p], to_up).start()

        @pl.when((z_ >= z) & (z > 0))
        def _():
            copy(x, y, z_, p, down_send, column_recv.at[z_, p], to_down).start()

        copy(x, y, z_, p, x_send, x_recv.at[z_, p], to_x).start()
        copy(x, y, z_, p, y_send, y_recv.at[z_, p], to_y).start()
        hand_on(x, y, z_, p)

    def from_plane(i):
        z_, p = nearest(i // PIECES), lax.rem(i, PIECES)
        copy(1 - x, y, z_, p, x_send, x_recv.at[z_, p], to_x).wait_recv()

        @pl.when(lax.rem(p, 2) == 0)
        def _():
            copy(1 - x, y, z_, p, y_send, diag_recv.at[z_, p], to_y).start()

        hand_on(1 - x, y, z_, p)
        copy(x, 1 - y, z_, p, y_send, y_recv.at[z_, p], to_y).wait_recv()

        @pl.when(lax.rem(p, 2) == 1)
        def _():
            copy(x, 1 - y, z_, p, x_send, diag_recv.at[z_, p], to_x).start()

        hand_on(x, 1 - y, z_, p)

    def from_diagonal(i):
        z_, p = nearest(i // PIECES), lax.rem(i, PIECES)
        copy(1 - x, 1 - y, z_, p, x_send, diag_recv.at[z_, p], to_x).wait_recv()
        hand_on(1 - x, 1 - y, z_, p)

    count = zs * PIECES

    @pl.loop(0, count + 2 * AHEAD)
    def _(i):
        @pl.when(i < count)
        def _():
            from_column(i)

        @pl.when((i >= AHEAD) & (i < count + AHEAD))
        def _():
            from_plane(i - AHEAD)

        @pl.when(i >= 2 * AHEAD)
        def _():
            from_diagonal(i - 2 * AHEAD)

    def drain(sem, blocks):
        view = blocks_ref.at[0, 0, pl.ds(0, blocks)]
        pltpu.make_async_copy(view, view, sem).wait()

    drain(x_send, zs + zs // 2)
    drain(y_send, zs + zs // 2)
    for at in range(zs):
        @pl.when(z == at)
        def _():
            if at < zs - 1:
                drain(up_send, at + 1)
            if at > 0:
                drain(down_send, zs - at)

    half = blocks_ref.at[0]
    pltpu.make_async_copy(half, half, core_send).wait()
    pltpu.make_async_copy(half, half, core_recv).wait()


def tile_kernel(rows_ref, cols_ref, row_block, col_block, out_ref):
    t = pl.program_id(0)
    slabs, variants = row_block.shape[1], row_block.shape[4]

    @pl.when(rows_ref[t] >= 0)
    def _():
        total = None
        for s in range(slabs):
            part = lax.dot_general(
                row_block[0, s, 0], col_block[0, s, 0], (((1,), (1,)), ((), ())),
                preferred_element_type=jnp.float32,
            )
            total = part if total is None else total + part
        out_ref[0] = total / (slabs * variants)

    @pl.when(rows_ref[t] < 0)
    def _():
        out_ref[...] = jnp.zeros_like(out_ref)


def fast(n, slabs, dosages, tile_rows, tile_cols):
    rows, variants = dosages.shape
    zs = n // 4
    dma = pltpu.SemaphoreType.DMA
    allele_freq, blocks = pl.pallas_call(
        functools.partial(gather_kernel, n),
        out_shape=(
            jax.ShapeDtypeStruct((1, variants), jnp.float32),
            jax.ShapeDtypeStruct((2, slabs, n // 2, rows, variants), jnp.bfloat16),
        ),
        in_specs=[pl.BlockSpec(memory_space=pltpu.VMEM)],
        out_specs=(pl.BlockSpec(memory_space=pltpu.VMEM), pl.BlockSpec(memory_space=pl.ANY)),
        scratch_shapes=[
            pltpu.VMEM((n, 1, variants), jnp.float32),
            pltpu.VMEM((rows, variants), jnp.bfloat16),
            dma((n,)), dma((n,)), dma,
            dma, dma, dma, dma, dma,
            dma((zs, PIECES)), dma((zs, PIECES)), dma((zs, PIECES)), dma((zs, PIECES)), dma,
        ],
        compiler_params=pltpu.CompilerParams(
            collective_id=0, has_side_effects=True, vmem_limit_bytes=32 * 1024 * 1024
        ),
    )(dosages)
    per_slab = tile_rows.shape[0] // slabs
    first = lax.axis_index("slab") * per_slab
    own_rows = lax.dynamic_slice_in_dim(tile_rows, first, per_slab, 0)
    own_cols = lax.dynamic_slice_in_dim(tile_cols, first, per_slab, 0)

    def place(t, rows_ref, cols_ref, which):
        block = jnp.maximum((rows_ref, cols_ref)[which][t], 0)
        return (lax.rem(block, 2), 0, block // 2, 0, 0)

    spec = lambda which: pl.BlockSpec(
        (1, slabs, 1, rows, variants), functools.partial(place, which=which)
    )
    grm_tiles = pl.pallas_call(
        tile_kernel,
        out_shape=jax.ShapeDtypeStruct((per_slab, rows, rows), jnp.float32),
        grid_spec=pltpu.PrefetchScalarGridSpec(
            num_scalar_prefetch=2,
            grid=(per_slab,),
            in_specs=[spec(0), spec(1)],
            out_specs=pl.BlockSpec((1, rows, rows), lambda t, r, c: (t, 0, 0)),
        ),
        compiler_params=pltpu.CompilerParams(vmem_limit_bytes=32 * 1024 * 1024),
    )(own_rows, own_cols, blocks, blocks)
    return allele_freq.reshape(variants), grm_tiles


def general(n, slabs, dosages, tile_rows, tile_cols):
    rows, variants = dosages.shape
    allele_freq, spread = frequencies(lax.psum(jnp.sum(dosages, axis=0), "ind"), rows * n)
    standard = ((dosages - 2.0 * allele_freq) * lax.rsqrt(spread)).astype(jnp.bfloat16)
    groups = lax.all_gather(standard, "ind", axis=0)
    row_blocks = groups[jnp.maximum(tile_rows, 0)]
    col_blocks = groups[jnp.maximum(tile_cols, 0)]
    per_slab = tile_rows.shape[0] // slabs
    first = lax.axis_index("slab") * per_slab
    listed = lax.dynamic_slice_in_dim(tile_rows, first, per_slab, 0) >= 0
    summed = lax.psum_scatter(
        jnp.einsum("krv,kcv->krc", row_blocks, col_blocks, preferred_element_type=jnp.float32),
        "slab", scatter_dimension=0, tiled=True,
    )
    return allele_freq, jnp.where(listed[:, None, None], summed / (variants * slabs), jnp.float32(0.0))


def solution(mesh):
    n, slabs = mesh.shape["ind"], mesh.shape["slab"]
    body = fast if slabs == 2 and n % 4 == 0 else general
    in_specs = (P("ind", "slab"), P("ind"), P("ind"))
    out_specs = (P("slab"), P(("ind", "slab"), None, None))
    return jax.shard_map(
        functools.partial(body, n, slabs),
        mesh=mesh, in_specs=in_specs, out_specs=out_specs, check_vma=False,
    )
```

```python
import functools

import jax
import jax.numpy as jnp
from jax import lax
from jax.experimental import pallas as pl
from jax.experimental.pallas import tpu as pltpu
from jax.sharding import PartitionSpec as P

MESH = pl.DeviceIdType.MESH
PIECES = 8
TURNED = 2
AHEAD = 6


def frequencies(total, people):
    allele_freq = total / (2.0 * people)
    spread = jnp.maximum(2.0 * allele_freq * (1.0 - allele_freq), 0.05)
    return allele_freq, spread


def gather_kernel(
    n, dosages_ref, freq_ref, blocks_ref,
    sums, own, sum_send, sum_recv, local_sem,
    x_send, y_send, up_send, down_send, core_send, recv, core_recv,
):
    rows, variants = own.shape
    zs = n // 4
    piece_rows = rows // PIECES
    me, x = lax.axis_index("ind"), lax.axis_index("slab")
    core, y, z = lax.rem(me, 2), lax.rem(me // 2, 2), me // 4

    def ind_of(z_, y_, core_):
        return (z_ * 2 + y_) * 2 + core_

    to_x = (me, 1 - x)
    to_y = (ind_of(z, 1 - y, core), x)
    to_core = (ind_of(z, y, 1 - core), x)
    to_up = (ind_of(jnp.minimum(z + 1, zs - 1), y, core), x)
    to_down = (ind_of(jnp.maximum(z - 1, 0), y, core), x)

    barrier = pltpu.get_barrier_semaphore()
    pl.semaphore_signal(barrier, inc=1, device_id=to_x, device_id_type=MESH)

    @pl.loop(1, n)
    def _(k):
        other = lax.rem(me + k, n)
        pl.semaphore_signal(barrier, inc=1, device_id=(other, x), device_id_type=MESH)

    sums[pl.ds(me, 1)] = jnp.sum(dosages_ref[...], axis=0).reshape(1, 1, variants)
    pl.semaphore_wait(barrier, n)

    def sum_copy(k, slot):
        other = lax.rem(me + k, n)
        return pltpu.make_async_remote_copy(
            src_ref=sums.at[slot], dst_ref=sums.at[slot],
            send_sem=sum_send.at[k], recv_sem=sum_recv.at[slot],
            device_id=(other, x), device_id_type=MESH,
        )

    @pl.loop(1, n)
    def _(k):
        sum_copy(k, me).start()

    @pl.loop(1, n)
    def _(k):
        sum_copy(k, lax.rem(me + k, n)).wait_recv()

    allele_freq, spread = frequencies(jnp.sum(sums[...], axis=0), rows * n)
    freq_ref[...] = allele_freq
    own[...] = ((dosages_ref[...] - 2.0 * allele_freq) * lax.rsqrt(spread)).astype(jnp.bfloat16)
    at = pl.multiple_of((z * 2 + y) * rows, rows)
    keep = pltpu.make_async_copy(own, blocks_ref.at[core, x, pl.ds(at, rows)], local_sem)
    keep.start()
    keep.wait()

    @pl.loop(1, n)
    def _(k):
        sum_copy(k, me).wait_send()

    def copy(x_, y_, z_, p, send_sem, to):
        at = pl.multiple_of(((z_ * 2 + y_) * PIECES + p) * piece_rows, piece_rows)
        part = blocks_ref.at[core, x_, pl.ds(at, piece_rows)]
        return pltpu.make_async_remote_copy(
            src_ref=part, dst_ref=part, send_sem=send_sem, recv_sem=recv.at[x_ * 2 + y_, z_, p],
            device_id=to, device_id_type=MESH,
        )

    def arrived(x_, y_, z_, p):
        copy(x_, y_, z_, p, x_send, to_x).wait_recv()

    def hand_on(x_, y_, z_, p):
        at = pl.multiple_of(((z_ * 2 + y_) * PIECES + p) * piece_rows, piece_rows)
        part = blocks_ref.at[core, x_, pl.ds(at, piece_rows)]
        pltpu.make_async_remote_copy(
            src_ref=part, dst_ref=part, send_sem=core_send, recv_sem=core_recv,
            device_id=to_core, device_id_type=MESH,
        ).start()

    def along_z(x_, y_, z_, p):
        @pl.when((z_ <= z) & (z < zs - 1))
        def _():
            copy(x_, y_, z_, p, up_send, to_up).start()

        @pl.when((z_ >= z) & (z > 0))
        def _():
            copy(x_, y_, z_, p, down_send, to_down).start()

    def nearest(step):
        near = jnp.minimum(z, zs - 1 - z)
        hop = (step + 1) // 2
        close = jnp.where(lax.rem(step, 2) == 1, z - hop, z + hop)
        far = jnp.where(z <= zs - 1 - z, step, zs - 1 - step)
        return jnp.where(step <= 2 * near, close, far)

    straight = PIECES - TURNED

    def from_column(i):
        z_, p = nearest(i // straight), lax.rem(i, straight)

        @pl.when(z_ != z)
        def _():
            arrived(x, y, z_, p)

        along_z(x, y, z_, p)
        copy(x, y, z_, p, x_send, to_x).start()
        copy(x, y, z_, p, y_send, to_y).start()
        hand_on(x, y, z_, p)

    def from_x(z_, p):
        arrived(1 - x, y, z_, p)

        @pl.when(lax.rem(p, 2) == 0)
        def _():
            copy(1 - x, y, z_, p, y_send, to_y).start()

    def from_y(z_, p):
        arrived(x, 1 - y, z_, p)

        @pl.when(lax.rem(p, 2) == 1)
        def _():
            copy(x, 1 - y, z_, p, x_send, to_x).start()

    def from_plane(i):
        z_, p = nearest(i // straight), lax.rem(i, straight)
        from_x(z_, p)
        hand_on(1 - x, y, z_, p)
        from_y(z_, p)
        hand_on(x, 1 - y, z_, p)

    def from_diagonal(i):
        z_, p = nearest(i // straight), lax.rem(i, straight)
        arrived(1 - x, 1 - y, z_, p)
        hand_on(1 - x, 1 - y, z_, p)

    def from_turned(j):
        z_, k, p = nearest(j // (4 * TURNED)), lax.rem(j // TURNED, 4), straight + lax.rem(j, TURNED)
        x_ = lax.rem(x + lax.rem(k, 2), 2)
        y_ = lax.rem(y + k // 2, 2)

        @pl.when((z_ == z) & (k == 1))
        def _():
            from_x(z, p)

        @pl.when((z_ == z) & (k == 2))
        def _():
            from_y(z, p)

        @pl.when((z_ != z) | (k == 3))
        def _():
            arrived(x_, y_, z_, p)

        along_z(x_, y_, z_, p)
        hand_on(x_, y_, z_, p)

    @pl.loop(straight, PIECES)
    def _(p):
        copy(x, y, z, p, x_send, to_x).start()
        copy(x, y, z, p, y_send, to_y).start()

    count = zs * straight
    turned = 4 * zs * TURNED

    @pl.loop(0, count + 2 * AHEAD)
    def _(i):
        @pl.when(i < count)
        def _():
            from_column(i)

        k = i - AHEAD

        @pl.when((k >= 0) & (k < count))
        def _():
            @pl.loop(k * turned // count, (k + 1) * turned // count)
            def _(j):
                from_turned(j)

            from_plane(k)

        @pl.when(i >= 2 * AHEAD)
        def _():
            from_diagonal(i - 2 * AHEAD)

    def drain(sem, pieces):
        view = blocks_ref.at[0, 0, pl.ds(0, pieces * piece_rows)]
        pltpu.make_async_copy(view, view, sem).wait()

    over = (zs * straight + TURNED) * 3 // 2
    drain(x_send, over)
    drain(y_send, over)
    for at in range(zs):
        @pl.when(z == at)
        def _():
            if at < zs - 1:
                drain(up_send, (at + 1) * (straight + 4 * TURNED))
            if at > 0:
                drain(down_send, (zs - at) * (straight + 4 * TURNED))

    half = blocks_ref.at[0]
    pltpu.make_async_copy(half, half, core_send).wait()
    pltpu.make_async_copy(half, half, core_recv).wait()


def tile_kernel(all_variants, rows_ref, cols_ref, row_block, col_block, out_ref):
    t = pl.program_id(0)

    @pl.when(rows_ref[t] >= 0)
    def _():
        total = None
        for s in range(row_block.shape[1]):
            part = lax.dot_general(
                row_block[0, s, 0], col_block[0, s, 0], (((1,), (1,)), ((), ())),
                preferred_element_type=jnp.float32,
            )
            total = part if total is None else total + part
        out_ref[0] = total / all_variants

    @pl.when(rows_ref[t] < 0)
    def _():
        out_ref[...] = jnp.zeros_like(out_ref)


def tiles(all_variants, blocks, tile_rows, tile_cols):
    cores, slabs, _, rows, variants = blocks.shape
    count = tile_rows.shape[0]

    def place(t, rows_ref, cols_ref, which):
        block = jnp.maximum((rows_ref, cols_ref)[which][t], 0)
        return (lax.rem(block, cores), 0, block // cores, 0, 0)

    spec = lambda which: pl.BlockSpec(
        (1, slabs, 1, rows, variants), functools.partial(place, which=which)
    )
    return pl.pallas_call(
        functools.partial(tile_kernel, all_variants),
        out_shape=jax.ShapeDtypeStruct((count, rows, rows), jnp.float32),
        grid_spec=pltpu.PrefetchScalarGridSpec(
            num_scalar_prefetch=2,
            grid=(count,),
            in_specs=[spec(0), spec(1)],
            out_specs=pl.BlockSpec((1, rows, rows), lambda t, r, c: (t, 0, 0)),
        ),
        compiler_params=pltpu.CompilerParams(vmem_limit_bytes=32 * 1024 * 1024),
    )(tile_rows, tile_cols, blocks, blocks)


def fast(n, slabs, dosages, tile_rows, tile_cols):
    rows, variants = dosages.shape
    zs = n // 4
    dma = pltpu.SemaphoreType.DMA
    allele_freq, blocks = pl.pallas_call(
        functools.partial(gather_kernel, n),
        out_shape=(
            jax.ShapeDtypeStruct((1, variants), jnp.float32),
            jax.ShapeDtypeStruct((2, slabs, n // 2 * rows, variants), jnp.bfloat16),
        ),
        in_specs=[pl.BlockSpec(memory_space=pltpu.VMEM)],
        out_specs=(pl.BlockSpec(memory_space=pltpu.VMEM), pl.BlockSpec(memory_space=pl.ANY)),
        scratch_shapes=[
            pltpu.VMEM((n, 1, variants), jnp.float32),
            pltpu.VMEM((rows, variants), jnp.bfloat16),
            dma((n,)), dma((n,)), dma,
            dma, dma, dma, dma, dma,
            dma((2 * slabs, zs, PIECES)), dma,
        ],
        compiler_params=pltpu.CompilerParams(
            collective_id=0, has_side_effects=True, vmem_limit_bytes=32 * 1024 * 1024
        ),
    )(dosages)
    per_slab = tile_rows.shape[0] // slabs
    first = lax.axis_index("slab") * per_slab
    own_rows = lax.dynamic_slice_in_dim(tile_rows, first, per_slab, 0)
    own_cols = lax.dynamic_slice_in_dim(tile_cols, first, per_slab, 0)

    grm_tiles = tiles(variants * slabs, blocks.reshape(2, slabs, n // 2, rows, variants), own_rows, own_cols)
    return allele_freq.reshape(variants), grm_tiles


def general(n, slabs, dosages, tile_rows, tile_cols):
    rows, variants = dosages.shape
    allele_freq, spread = frequencies(lax.psum(jnp.sum(dosages, axis=0), "ind"), rows * n)
    standard = ((dosages - 2.0 * allele_freq) * lax.rsqrt(spread)).astype(jnp.bfloat16)
    groups = lax.all_gather(standard, "ind", axis=0)
    shares = tiles(variants * slabs, groups[None, None], tile_rows, tile_cols)
    return allele_freq, lax.psum_scatter(shares, "slab", scatter_dimension=0, tiled=True)


def solution(mesh):
    n, slabs = mesh.shape["ind"], mesh.shape["slab"]
    body = fast if slabs == 2 and n % 4 == 0 else general
    in_specs = (P("ind", "slab"), P("ind"), P("ind"))
    out_specs = (P("slab"), P(("ind", "slab"), None, None))
    return jax.shard_map(
        functools.partial(body, n, slabs),
        mesh=mesh, in_specs=in_specs, out_specs=out_specs, check_vma=False,
    )
```

```python
import functools

import jax
import jax.numpy as jnp
from jax import lax
from jax.experimental import pallas as pl
from jax.experimental.pallas import tpu as pltpu
from jax.sharding import PartitionSpec as P

MESH = pl.DeviceIdType.MESH
PIECES = 8
TURNED = 2
AHEAD = 3
LATE = 10


def frequencies(total, people):
    allele_freq = total / (2.0 * people)
    spread = jnp.maximum(2.0 * allele_freq * (1.0 - allele_freq), 0.05)
    return allele_freq, spread


def gather_kernel(
    n, dosages_ref, freq_ref, blocks_ref,
    sums, own, sum_send, sum_recv, local_sem,
    x_send, y_send, up_send, down_send, core_send, recv, core_recv,
):
    rows, variants = own.shape
    zs = n // 4
    piece_rows = rows // PIECES
    me, x = lax.axis_index("ind"), lax.axis_index("slab")
    core, y, z = lax.rem(me, 2), lax.rem(me // 2, 2), me // 4

    def ind_of(z_, y_, core_):
        return (z_ * 2 + y_) * 2 + core_

    to_x = (me, 1 - x)
    to_y = (ind_of(z, 1 - y, core), x)
    to_core = (ind_of(z, y, 1 - core), x)
    to_up = (ind_of(jnp.minimum(z + 1, zs - 1), y, core), x)
    to_down = (ind_of(jnp.maximum(z - 1, 0), y, core), x)

    barrier = pltpu.get_barrier_semaphore()
    pl.semaphore_signal(barrier, inc=1, device_id=to_x, device_id_type=MESH)

    @pl.loop(1, n)
    def _(k):
        other = lax.rem(me + k, n)
        pl.semaphore_signal(barrier, inc=1, device_id=(other, x), device_id_type=MESH)

    sums[pl.ds(me, 1)] = jnp.sum(dosages_ref[...], axis=0).reshape(1, 1, variants)
    pl.semaphore_wait(barrier, n)

    def sum_copy(k, slot):
        other = lax.rem(me + k, n)
        return pltpu.make_async_remote_copy(
            src_ref=sums.at[slot], dst_ref=sums.at[slot],
            send_sem=sum_send.at[k], recv_sem=sum_recv.at[slot],
            device_id=(other, x), device_id_type=MESH,
        )

    @pl.loop(1, n)
    def _(k):
        sum_copy(k, me).start()

    @pl.loop(1, n)
    def _(k):
        sum_copy(k, lax.rem(me + k, n)).wait_recv()

    allele_freq, spread = frequencies(jnp.sum(sums[...], axis=0), rows * n)
    freq_ref[...] = allele_freq
    own[...] = ((dosages_ref[...] - 2.0 * allele_freq) * lax.rsqrt(spread)).astype(jnp.bfloat16)
    at = pl.multiple_of((z * 2 + y) * rows, rows)
    keep = pltpu.make_async_copy(own, blocks_ref.at[core, x, pl.ds(at, rows)], local_sem)
    keep.start()
    keep.wait()

    @pl.loop(1, n)
    def _(k):
        sum_copy(k, me).wait_send()

    def copy(x_, y_, z_, p, send_sem, to):
        at = pl.multiple_of(((z_ * 2 + y_) * PIECES + p) * piece_rows, piece_rows)
        part = blocks_ref.at[core, x_, pl.ds(at, piece_rows)]
        return pltpu.make_async_remote_copy(
            src_ref=part, dst_ref=part, send_sem=send_sem, recv_sem=recv.at[x_ * 2 + y_, z_, p],
            device_id=to, device_id_type=MESH,
        )

    def arrived(x_, y_, z_, p):
        copy(x_, y_, z_, p, x_send, to_x).wait_recv()

    def hand_on(x_, y_, z_, p):
        at = pl.multiple_of(((z_ * 2 + y_) * PIECES + p) * piece_rows, piece_rows)
        part = blocks_ref.at[core, x_, pl.ds(at, piece_rows)]
        pltpu.make_async_remote_copy(
            src_ref=part, dst_ref=part, send_sem=core_send, recv_sem=core_recv,
            device_id=to_core, device_id_type=MESH,
        ).start()

    def along_z(x_, y_, z_, p):
        @pl.when((z_ <= z) & (z < zs - 1))
        def _():
            copy(x_, y_, z_, p, up_send, to_up).start()

        @pl.when((z_ >= z) & (z > 0))
        def _():
            copy(x_, y_, z_, p, down_send, to_down).start()

    straight = PIECES - TURNED
    count = zs * straight
    first = (zs - 1) * straight
    slots = first + (zs - 1) * 4 * TURNED

    def nth(i):
        m = i - straight
        both = jnp.minimum(z, zs - 1 - z) * 2 * straight
        q = lax.rem(m, 2 * straight)
        hop = m // (2 * straight) + 1
        near = jnp.where(lax.rem(q, 2) == 0, z - hop, z + hop)
        rest = m - both
        hop = jnp.minimum(z, zs - 1 - z) + 1 + rest // straight
        far = jnp.where(z <= zs - 1 - z, z + hop, z - hop)
        z_ = jnp.where(m < 0, z, jnp.where(m < both, near, far))
        p = jnp.where(m < 0, i, jnp.where(m < both, q // 2, lax.rem(rest, straight)))
        return z_, p

    def straight_on(z_, p):
        along_z(x, y, z_, p)
        copy(x, y, z_, p, x_send, to_x).start()
        copy(x, y, z_, p, y_send, to_y).start()
        hand_on(x, y, z_, p)

    def corner(j):
        k = lax.rem(j // TURNED, 4)
        return lax.rem(x + lax.rem(k, 2), 2), lax.rem(y + k // 2, 2), straight + lax.rem(j, TURNED)

    def along(k, sign):
        @pl.when(k < first)
        def _():
            z_ = z + sign * (k // straight + 1)

            @pl.when((z_ >= 0) & (z_ < zs))
            def _():
                p = lax.rem(k, straight)
                arrived(x, y, z_, p)
                straight_on(z_, p)

        @pl.when(k >= first)
        def _():
            j = k - first
            z_ = z + sign * (j // (4 * TURNED) + 1)

            @pl.when((z_ >= 0) & (z_ < zs))
            def _():
                x_, y_, p = corner(j)
                arrived(x_, y_, z_, p)
                along_z(x_, y_, z_, p)
                hand_on(x_, y_, z_, p)

    def from_x(z_, p):
        arrived(1 - x, y, z_, p)

        @pl.when(lax.rem(p, 2) == 0)
        def _():
            copy(1 - x, y, z_, p, y_send, to_y).start()

    def from_y(z_, p):
        arrived(x, 1 - y, z_, p)

        @pl.when(lax.rem(p, 2) == 1)
        def _():
            copy(x, 1 - y, z_, p, x_send, to_x).start()

    def from_plane(i):
        z_, p = nth(i)
        from_x(z_, p)
        hand_on(1 - x, y, z_, p)
        from_y(z_, p)
        hand_on(x, 1 - y, z_, p)

    def from_diagonal(i):
        z_, p = nth(i)
        arrived(1 - x, 1 - y, z_, p)
        hand_on(1 - x, 1 - y, z_, p)

    @pl.loop(straight, PIECES)
    def _(p):
        copy(x, y, z, p, x_send, to_x).start()
        copy(x, y, z, p, y_send, to_y).start()

    @pl.loop(0, straight)
    def _(p):
        straight_on(z, p)

    @pl.loop(0, count + LATE)
    def _(i):
        now = jnp.minimum(i, count)
        later = jnp.minimum(i + 1, count)

        @pl.loop(now * slots // count, later * slots // count)
        def _(k):
            along(k, -1)
            along(k, 1)

            @pl.when(k == first // 2)
            def _():
                @pl.loop(0, 4 * TURNED)
                def _(j):
                    x_, y_, p = corner(j)

                    @pl.when(j // TURNED == 1)
                    def _():
                        from_x(z, p)

                    @pl.when(j // TURNED == 2)
                    def _():
                        from_y(z, p)

            @pl.when(k == first - TURNED)
            def _():
                @pl.loop(0, 4 * TURNED)
                def _(j):
                    x_, y_, p = corner(j)

                    @pl.when(j // TURNED == 3)
                    def _():
                        arrived(x_, y_, z, p)

                    along_z(x_, y_, z, p)
                    hand_on(x_, y_, z, p)

        @pl.when((i >= AHEAD) & (i < count + AHEAD))
        def _():
            from_plane(i - AHEAD)

        @pl.when(i >= LATE)
        def _():
            from_diagonal(i - LATE)

    def drain(sem, pieces):
        view = blocks_ref.at[0, 0, pl.ds(0, pieces * piece_rows)]
        pltpu.make_async_copy(view, view, sem).wait()

    over = (zs * straight + TURNED) * 3 // 2
    drain(x_send, over)
    drain(y_send, over)
    for at in range(zs):
        @pl.when(z == at)
        def _():
            if at < zs - 1:
                drain(up_send, (at + 1) * (straight + 4 * TURNED))
            if at > 0:
                drain(down_send, (zs - at) * (straight + 4 * TURNED))

    half = blocks_ref.at[0]
    pltpu.make_async_copy(half, half, core_send).wait()
    pltpu.make_async_copy(half, half, core_recv).wait()


def tile_kernel(all_variants, rows_ref, cols_ref, row_block, col_block, out_ref):
    t = pl.program_id(0)

    @pl.when(rows_ref[t] >= 0)
    def _():
        total = None
        for s in range(row_block.shape[1]):
            part = lax.dot_general(
                row_block[0, s, 0], col_block[0, s, 0], (((1,), (1,)), ((), ())),
                preferred_element_type=jnp.float32,
            )
            total = part if total is None else total + part
        out_ref[0] = total / all_variants

    @pl.when(rows_ref[t] < 0)
    def _():
        out_ref[...] = jnp.zeros_like(out_ref)


def tiles(all_variants, blocks, tile_rows, tile_cols):
    cores, slabs, _, rows, variants = blocks.shape
    count = tile_rows.shape[0]

    def place(t, rows_ref, cols_ref, which):
        block = jnp.maximum((rows_ref, cols_ref)[which][t], 0)
        return (lax.rem(block, cores), 0, block // cores, 0, 0)

    spec = lambda which: pl.BlockSpec(
        (1, slabs, 1, rows, variants), functools.partial(place, which=which)
    )
    return pl.pallas_call(
        functools.partial(tile_kernel, all_variants),
        out_shape=jax.ShapeDtypeStruct((count, rows, rows), jnp.float32),
        grid_spec=pltpu.PrefetchScalarGridSpec(
            num_scalar_prefetch=2,
            grid=(count,),
            in_specs=[spec(0), spec(1)],
            out_specs=pl.BlockSpec((1, rows, rows), lambda t, r, c: (t, 0, 0)),
        ),
        compiler_params=pltpu.CompilerParams(vmem_limit_bytes=32 * 1024 * 1024),
    )(tile_rows, tile_cols, blocks, blocks)


def fast(n, slabs, dosages, tile_rows, tile_cols):
    rows, variants = dosages.shape
    zs = n // 4
    dma = pltpu.SemaphoreType.DMA
    allele_freq, blocks = pl.pallas_call(
        functools.partial(gather_kernel, n),
        out_shape=(
            jax.ShapeDtypeStruct((1, variants), jnp.float32),
            jax.ShapeDtypeStruct((2, slabs, n // 2 * rows, variants), jnp.bfloat16),
        ),
        in_specs=[pl.BlockSpec(memory_space=pltpu.VMEM)],
        out_specs=(pl.BlockSpec(memory_space=pltpu.VMEM), pl.BlockSpec(memory_space=pl.ANY)),
        scratch_shapes=[
            pltpu.VMEM((n, 1, variants), jnp.float32),
            pltpu.VMEM((rows, variants), jnp.bfloat16),
            dma((n,)), dma((n,)), dma,
            dma, dma, dma, dma, dma,
            dma((2 * slabs, zs, PIECES)), dma,
        ],
        compiler_params=pltpu.CompilerParams(
            collective_id=0, has_side_effects=True, vmem_limit_bytes=32 * 1024 * 1024
        ),
    )(dosages)
    per_slab = tile_rows.shape[0] // slabs
    first = lax.axis_index("slab") * per_slab
    own_rows = lax.dynamic_slice_in_dim(tile_rows, first, per_slab, 0)
    own_cols = lax.dynamic_slice_in_dim(tile_cols, first, per_slab, 0)

    grm_tiles = tiles(variants * slabs, blocks.reshape(2, slabs, n // 2, rows, variants), own_rows, own_cols)
    return allele_freq.reshape(variants), grm_tiles


def general(n, slabs, dosages, tile_rows, tile_cols):
    rows, variants = dosages.shape
    allele_freq, spread = frequencies(lax.psum(jnp.sum(dosages, axis=0), "ind"), rows * n)
    standard = ((dosages - 2.0 * allele_freq) * lax.rsqrt(spread)).astype(jnp.bfloat16)
    groups = lax.all_gather(standard, "ind", axis=0)
    shares = tiles(variants * slabs, groups[None, None], tile_rows, tile_cols)
    return allele_freq, lax.psum_scatter(shares, "slab", scatter_dimension=0, tiled=True)


def solution(mesh):
    n, slabs = mesh.shape["ind"], mesh.shape["slab"]
    body = fast if slabs == 2 and n % 4 == 0 else general
    in_specs = (P("ind", "slab"), P("ind"), P("ind"))
    out_specs = (P("slab"), P(("ind", "slab"), None, None))
    return jax.shard_map(
        functools.partial(body, n, slabs),
        mesh=mesh, in_specs=in_specs, out_specs=out_specs, check_vma=False,
    )
```

```python
import functools

import jax
import jax.numpy as jnp
from jax import lax
from jax.experimental import pallas as pl
from jax.experimental.pallas import tpu as pltpu
from jax.sharding import PartitionSpec as P

MESH = pl.DeviceIdType.MESH
PIECES = 16
TURNED = 2
AHEAD = 6
LATE = 20


def frequencies(total, people):
    allele_freq = total / (2.0 * people)
    spread = jnp.maximum(2.0 * allele_freq * (1.0 - allele_freq), 0.05)
    return allele_freq, spread


def gather_kernel(
    n, dosages_ref, freq_ref, blocks_ref,
    sums, own, sum_send, sum_recv, local_sem,
    x_send, y_send, up_send, down_send, core_send, recv, core_recv,
):
    rows, variants = own.shape
    zs = n // 4
    piece_rows = rows // PIECES
    me, x = lax.axis_index("ind"), lax.axis_index("slab")
    core, y, z = lax.rem(me, 2), lax.rem(me // 2, 2), me // 4

    def ind_of(z_, y_, core_):
        return (z_ * 2 + y_) * 2 + core_

    to_x = (me, 1 - x)
    to_y = (ind_of(z, 1 - y, core), x)
    to_core = (ind_of(z, y, 1 - core), x)
    to_up = (ind_of(jnp.minimum(z + 1, zs - 1), y, core), x)
    to_down = (ind_of(jnp.maximum(z - 1, 0), y, core), x)

    barrier = pltpu.get_barrier_semaphore()
    pl.semaphore_signal(barrier, inc=1, device_id=to_x, device_id_type=MESH)

    @pl.loop(1, n)
    def _(k):
        other = lax.rem(me + k, n)
        pl.semaphore_signal(barrier, inc=1, device_id=(other, x), device_id_type=MESH)

    sums[pl.ds(me, 1)] = jnp.sum(dosages_ref[...], axis=0).reshape(1, 1, variants)
    pl.semaphore_wait(barrier, n)

    def sum_copy(k, slot):
        other = lax.rem(me + k, n)
        return pltpu.make_async_remote_copy(
            src_ref=sums.at[slot], dst_ref=sums.at[slot],
            send_sem=sum_send.at[k], recv_sem=sum_recv.at[slot],
            device_id=(other, x), device_id_type=MESH,
        )

    @pl.loop(1, n)
    def _(k):
        sum_copy(k, me).start()

    @pl.loop(1, n)
    def _(k):
        sum_copy(k, lax.rem(me + k, n)).wait_recv()

    allele_freq, spread = frequencies(jnp.sum(sums[...], axis=0), rows * n)
    freq_ref[...] = allele_freq
    own[...] = ((dosages_ref[...] - 2.0 * allele_freq) * lax.rsqrt(spread)).astype(jnp.bfloat16)
    at = pl.multiple_of((z * 2 + y) * rows, rows)
    keep = pltpu.make_async_copy(own, blocks_ref.at[core, x, pl.ds(at, rows)], local_sem)
    keep.start()
    keep.wait()

    @pl.loop(1, n)
    def _(k):
        sum_copy(k, me).wait_send()

    def copy(x_, y_, z_, p, send_sem, to):
        at = pl.multiple_of(((z_ * 2 + y_) * PIECES + p) * piece_rows, piece_rows)
        part = blocks_ref.at[core, x_, pl.ds(at, piece_rows)]
        return pltpu.make_async_remote_copy(
            src_ref=part, dst_ref=part, send_sem=send_sem, recv_sem=recv.at[x_ * 2 + y_, z_, p],
            device_id=to, device_id_type=MESH,
        )

    def arrived(x_, y_, z_, p):
        copy(x_, y_, z_, p, x_send, to_x).wait_recv()

    def hand_on(x_, y_, z_, p):
        at = pl.multiple_of(((z_ * 2 + y_) * PIECES + p) * piece_rows, piece_rows)
        part = blocks_ref.at[core, x_, pl.ds(at, piece_rows)]
        pltpu.make_async_remote_copy(
            src_ref=part, dst_ref=part, send_sem=core_send, recv_sem=core_recv,
            device_id=to_core, device_id_type=MESH,
        ).start()

    def along_z(x_, y_, z_, p):
        @pl.when((z_ <= z) & (z < zs - 1))
        def _():
            copy(x_, y_, z_, p, up_send, to_up).start()

        @pl.when((z_ >= z) & (z > 0))
        def _():
            copy(x_, y_, z_, p, down_send, to_down).start()

    straight = PIECES - TURNED
    count = zs * straight
    first = (zs - 1) * straight
    slots = first + (zs - 1) * 4 * TURNED

    def nth(i):
        m = i - straight
        both = jnp.minimum(z, zs - 1 - z) * 2 * straight
        q = lax.rem(m, 2 * straight)
        hop = m // (2 * straight) + 1
        near = jnp.where(lax.rem(q, 2) == 0, z - hop, z + hop)
        rest = m - both
        hop = jnp.minimum(z, zs - 1 - z) + 1 + rest // straight
        far = jnp.where(z <= zs - 1 - z, z + hop, z - hop)
        z_ = jnp.where(m < 0, z, jnp.where(m < both, near, far))
        p = jnp.where(m < 0, i, jnp.where(m < both, q // 2, lax.rem(rest, straight)))
        return z_, p

    def straight_on(z_, p):
        along_z(x, y, z_, p)
        copy(x, y, z_, p, x_send, to_x).start()
        copy(x, y, z_, p, y_send, to_y).start()
        hand_on(x, y, z_, p)

    def corner(j):
        k = lax.rem(j // TURNED, 4)
        return lax.rem(x + lax.rem(k, 2), 2), lax.rem(y + k // 2, 2), straight + lax.rem(j, TURNED)

    def along(k, sign):
        @pl.when(k < first)
        def _():
            z_ = z + sign * (k // straight + 1)

            @pl.when((z_ >= 0) & (z_ < zs))
            def _():
                p = lax.rem(k, straight)
                arrived(x, y, z_, p)
                straight_on(z_, p)

        @pl.when(k >= first)
        def _():
            j = k - first
            z_ = z + sign * (j // (4 * TURNED) + 1)

            @pl.when((z_ >= 0) & (z_ < zs))
            def _():
                x_, y_, p = corner(j)
                arrived(x_, y_, z_, p)
                along_z(x_, y_, z_, p)
                hand_on(x_, y_, z_, p)

    def from_x(z_, p):
        arrived(1 - x, y, z_, p)

        @pl.when(lax.rem(p, 2) == 0)
        def _():
            copy(1 - x, y, z_, p, y_send, to_y).start()

    def from_y(z_, p):
        arrived(x, 1 - y, z_, p)

        @pl.when(lax.rem(p, 2) == 1)
        def _():
            copy(x, 1 - y, z_, p, x_send, to_x).start()

    def from_plane(i):
        z_, p = nth(i)
        from_x(z_, p)
        hand_on(1 - x, y, z_, p)
        from_y(z_, p)
        hand_on(x, 1 - y, z_, p)

    def from_diagonal(i):
        z_, p = nth(i)
        arrived(1 - x, 1 - y, z_, p)
        hand_on(1 - x, 1 - y, z_, p)

    @pl.loop(straight, PIECES)
    def _(p):
        copy(x, y, z, p, x_send, to_x).start()
        copy(x, y, z, p, y_send, to_y).start()

    @pl.loop(0, straight)
    def _(p):
        straight_on(z, p)

    @pl.loop(0, count + LATE)
    def _(i):
        now = jnp.minimum(i, count)
        later = jnp.minimum(i + 1, count)

        @pl.loop(now * slots // count, later * slots // count)
        def _(k):
            along(k, -1)
            along(k, 1)

            @pl.when(k == first // 2)
            def _():
                @pl.loop(0, 4 * TURNED)
                def _(j):
                    x_, y_, p = corner(j)

                    @pl.when(j // TURNED == 1)
                    def _():
                        from_x(z, p)

                    @pl.when(j // TURNED == 2)
                    def _():
                        from_y(z, p)

            @pl.when(k == first - TURNED)
            def _():
                @pl.loop(0, 4 * TURNED)
                def _(j):
                    x_, y_, p = corner(j)

                    @pl.when(j // TURNED == 3)
                    def _():
                        arrived(x_, y_, z, p)

                    along_z(x_, y_, z, p)
                    hand_on(x_, y_, z, p)

        @pl.when((i >= AHEAD) & (i < count + AHEAD))
        def _():
            from_plane(i - AHEAD)

        @pl.when(i >= LATE)
        def _():
            from_diagonal(i - LATE)

    def drain(sem, pieces):
        view = blocks_ref.at[0, 0, pl.ds(0, pieces * piece_rows)]
        pltpu.make_async_copy(view, view, sem).wait()

    over = (zs * straight + TURNED) * 3 // 2
    drain(x_send, over)
    drain(y_send, over)
    for at in range(zs):
        @pl.when(z == at)
        def _():
            if at < zs - 1:
                drain(up_send, (at + 1) * (straight + 4 * TURNED))
            if at > 0:
                drain(down_send, (zs - at) * (straight + 4 * TURNED))

    half = blocks_ref.at[0]
    pltpu.make_async_copy(half, half, core_send).wait()
    pltpu.make_async_copy(half, half, core_recv).wait()


def tile_kernel(all_variants, rows_ref, cols_ref, row_block, col_block, out_ref):
    t = pl.program_id(0)

    @pl.when(rows_ref[t] >= 0)
    def _():
        total = None
        for s in range(row_block.shape[1]):
            part = lax.dot_general(
                row_block[0, s, 0], col_block[0, s, 0], (((1,), (1,)), ((), ())),
                preferred_element_type=jnp.float32,
            )
            total = part if total is None else total + part
        out_ref[0] = total / all_variants

    @pl.when(rows_ref[t] < 0)
    def _():
        out_ref[...] = jnp.zeros_like(out_ref)


def tiles(all_variants, blocks, tile_rows, tile_cols):
    cores, slabs, _, rows, variants = blocks.shape
    count = tile_rows.shape[0]

    def place(t, rows_ref, cols_ref, which):
        block = jnp.maximum((rows_ref, cols_ref)[which][t], 0)
        return (lax.rem(block, cores), 0, block // cores, 0, 0)

    spec = lambda which: pl.BlockSpec(
        (1, slabs, 1, rows, variants), functools.partial(place, which=which)
    )
    return pl.pallas_call(
        functools.partial(tile_kernel, all_variants),
        out_shape=jax.ShapeDtypeStruct((count, rows, rows), jnp.float32),
        grid_spec=pltpu.PrefetchScalarGridSpec(
            num_scalar_prefetch=2,
            grid=(count,),
            in_specs=[spec(0), spec(1)],
            out_specs=pl.BlockSpec((1, rows, rows), lambda t, r, c: (t, 0, 0)),
        ),
        compiler_params=pltpu.CompilerParams(vmem_limit_bytes=32 * 1024 * 1024),
    )(tile_rows, tile_cols, blocks, blocks)


def fast(n, slabs, dosages, tile_rows, tile_cols):
    rows, variants = dosages.shape
    zs = n // 4
    dma = pltpu.SemaphoreType.DMA
    allele_freq, blocks = pl.pallas_call(
        functools.partial(gather_kernel, n),
        out_shape=(
            jax.ShapeDtypeStruct((1, variants), jnp.float32),
            jax.ShapeDtypeStruct((2, slabs, n // 2 * rows, variants), jnp.bfloat16),
        ),
        in_specs=[pl.BlockSpec(memory_space=pltpu.VMEM)],
        out_specs=(pl.BlockSpec(memory_space=pltpu.VMEM), pl.BlockSpec(memory_space=pl.ANY)),
        scratch_shapes=[
            pltpu.VMEM((n, 1, variants), jnp.float32),
            pltpu.VMEM((rows, variants), jnp.bfloat16),
            dma((n,)), dma((n,)), dma,
            dma, dma, dma, dma, dma,
            dma((2 * slabs, zs, PIECES)), dma,
        ],
        compiler_params=pltpu.CompilerParams(
            collective_id=0, has_side_effects=True, vmem_limit_bytes=32 * 1024 * 1024
        ),
    )(dosages)
    per_slab = tile_rows.shape[0] // slabs
    first = lax.axis_index("slab") * per_slab
    own_rows = lax.dynamic_slice_in_dim(tile_rows, first, per_slab, 0)
    own_cols = lax.dynamic_slice_in_dim(tile_cols, first, per_slab, 0)

    grm_tiles = tiles(variants * slabs, blocks.reshape(2, slabs, n // 2, rows, variants), own_rows, own_cols)
    return allele_freq.reshape(variants), grm_tiles


def general(n, slabs, dosages, tile_rows, tile_cols):
    rows, variants = dosages.shape
    allele_freq, spread = frequencies(lax.psum(jnp.sum(dosages, axis=0), "ind"), rows * n)
    standard = ((dosages - 2.0 * allele_freq) * lax.rsqrt(spread)).astype(jnp.bfloat16)
    groups = lax.all_gather(standard, "ind", axis=0)
    shares = tiles(variants * slabs, groups[None, None], tile_rows, tile_cols)
    return allele_freq, lax.psum_scatter(shares, "slab", scatter_dimension=0, tiled=True)


def solution(mesh):
    n, slabs = mesh.shape["ind"], mesh.shape["slab"]
    body = fast if slabs == 2 and n % 4 == 0 else general
    in_specs = (P("ind", "slab"), P("ind"), P("ind"))
    out_specs = (P("slab"), P(("ind", "slab"), None, None))
    return jax.shard_map(
        functools.partial(body, n, slabs),
        mesh=mesh, in_specs=in_specs, out_specs=out_specs, check_vma=False,
    )
```

```python
import functools

import jax
import jax.numpy as jnp
from jax import lax
from jax.experimental import pallas as pl
from jax.experimental.pallas import tpu as pltpu
from jax.sharding import PartitionSpec as P

MESH = pl.DeviceIdType.MESH
PIECES = 16
TURNED = 2
AHEAD = 6
LATE = 20


def frequencies(total, people):
    allele_freq = total / (2.0 * people)
    spread = jnp.maximum(2.0 * allele_freq * (1.0 - allele_freq), 0.05)
    return allele_freq, spread


def gather_kernel(
    n, given_ref, freq_ref, blocks_ref,
    dosages_ref, sums, own, sum_send, sum_recv, local_sem,
    x_send, y_send, up_send, down_send, core_send, recv, core_recv,
):
    rows, variants = own.shape
    zs = n // 4
    piece_rows = rows // PIECES
    me, x = lax.axis_index("ind"), lax.axis_index("slab")
    core, y, z = lax.rem(me, 2), lax.rem(me // 2, 2), me // 4

    def ind_of(z_, y_, core_):
        return (z_ * 2 + y_) * 2 + core_

    to_x = (me, 1 - x)
    to_y = (ind_of(z, 1 - y, core), x)
    to_core = (ind_of(z, y, 1 - core), x)
    to_up = (ind_of(jnp.minimum(z + 1, zs - 1), y, core), x)
    to_down = (ind_of(jnp.maximum(z - 1, 0), y, core), x)

    fetch = pltpu.make_async_copy(given_ref, dosages_ref, local_sem)
    fetch.start()
    barrier = pltpu.get_barrier_semaphore()
    pl.semaphore_signal(barrier, inc=1, device_id=to_x, device_id_type=MESH)

    @pl.loop(1, n)
    def _(k):
        other = lax.rem(me + k, n)
        pl.semaphore_signal(barrier, inc=1, device_id=(other, x), device_id_type=MESH)

    fetch.wait()
    sums[pl.ds(me, 1)] = jnp.sum(dosages_ref[...], axis=0).reshape(1, 1, variants)
    pl.semaphore_wait(barrier, n)

    def sum_copy(k, slot):
        other = lax.rem(me + k, n)
        return pltpu.make_async_remote_copy(
            src_ref=sums.at[slot], dst_ref=sums.at[slot],
            send_sem=sum_send.at[k], recv_sem=sum_recv.at[slot],
            device_id=(other, x), device_id_type=MESH,
        )

    @pl.loop(1, n)
    def _(k):
        sum_copy(k, me).start()

    @pl.loop(1, n)
    def _(k):
        sum_copy(k, lax.rem(me + k, n)).wait_recv()

    allele_freq, spread = frequencies(jnp.sum(sums[...], axis=0), rows * n)
    freq_ref[...] = allele_freq
    own[...] = ((dosages_ref[...] - 2.0 * allele_freq) * lax.rsqrt(spread)).astype(jnp.bfloat16)
    at = pl.multiple_of((z * 2 + y) * rows, rows)
    keep = pltpu.make_async_copy(own, blocks_ref.at[core, x, pl.ds(at, rows)], local_sem)
    keep.start()
    keep.wait()

    @pl.loop(1, n)
    def _(k):
        sum_copy(k, me).wait_send()

    def copy(x_, y_, z_, p, send_sem, to):
        at = pl.multiple_of(((z_ * 2 + y_) * PIECES + p) * piece_rows, piece_rows)
        part = blocks_ref.at[core, x_, pl.ds(at, piece_rows)]
        return pltpu.make_async_remote_copy(
            src_ref=part, dst_ref=part, send_sem=send_sem, recv_sem=recv.at[x_ * 2 + y_, z_, p],
            device_id=to, device_id_type=MESH,
        )

    def arrived(x_, y_, z_, p):
        copy(x_, y_, z_, p, x_send, to_x).wait_recv()

    def hand_on(x_, y_, z_, p):
        at = pl.multiple_of(((z_ * 2 + y_) * PIECES + p) * piece_rows, piece_rows)
        part = blocks_ref.at[core, x_, pl.ds(at, piece_rows)]
        pltpu.make_async_remote_copy(
            src_ref=part, dst_ref=part, send_sem=core_send, recv_sem=core_recv,
            device_id=to_core, device_id_type=MESH,
        ).start()

    def along_z(x_, y_, z_, p):
        @pl.when((z_ <= z) & (z < zs - 1))
        def _():
            copy(x_, y_, z_, p, up_send, to_up).start()

        @pl.when((z_ >= z) & (z > 0))
        def _():
            copy(x_, y_, z_, p, down_send, to_down).start()

    straight = PIECES - TURNED
    count = zs * straight
    first = (zs - 1) * straight
    slots = first + (zs - 1) * 4 * TURNED

    def nth(i):
        m = i - straight
        both = jnp.minimum(z, zs - 1 - z) * 2 * straight
        q = lax.rem(m, 2 * straight)
        hop = m // (2 * straight) + 1
        near = jnp.where(lax.rem(q, 2) == 0, z - hop, z + hop)
        rest = m - both
        hop = jnp.minimum(z, zs - 1 - z) + 1 + rest // straight
        far = jnp.where(z <= zs - 1 - z, z + hop, z - hop)
        z_ = jnp.where(m < 0, z, jnp.where(m < both, near, far))
        p = jnp.where(m < 0, i, jnp.where(m < both, q // 2, lax.rem(rest, straight)))
        return z_, p

    def straight_on(z_, p):
        along_z(x, y, z_, p)
        copy(x, y, z_, p, x_send, to_x).start()
        copy(x, y, z_, p, y_send, to_y).start()
        hand_on(x, y, z_, p)

    def corner(j):
        k = lax.rem(j // TURNED, 4)
        return lax.rem(x + lax.rem(k, 2), 2), lax.rem(y + k // 2, 2), straight + lax.rem(j, TURNED)

    def along(k, sign):
        @pl.when(k < first)
        def _():
            z_ = z + sign * (k // straight + 1)

            @pl.when((z_ >= 0) & (z_ < zs))
            def _():
                p = lax.rem(k, straight)
                arrived(x, y, z_, p)
                straight_on(z_, p)

        @pl.when(k >= first)
        def _():
            j = k - first
            z_ = z + sign * (j // (4 * TURNED) + 1)

            @pl.when((z_ >= 0) & (z_ < zs))
            def _():
                x_, y_, p = corner(j)
                arrived(x_, y_, z_, p)
                along_z(x_, y_, z_, p)
                hand_on(x_, y_, z_, p)

    def from_x(z_, p):
        arrived(1 - x, y, z_, p)

        @pl.when(lax.rem(p, 2) == 0)
        def _():
            copy(1 - x, y, z_, p, y_send, to_y).start()

    def from_y(z_, p):
        arrived(x, 1 - y, z_, p)

        @pl.when(lax.rem(p, 2) == 1)
        def _():
            copy(x, 1 - y, z_, p, x_send, to_x).start()

    def from_plane(i):
        z_, p = nth(i)
        from_x(z_, p)
        hand_on(1 - x, y, z_, p)
        from_y(z_, p)
        hand_on(x, 1 - y, z_, p)

    def from_diagonal(i):
        z_, p = nth(i)
        arrived(1 - x, 1 - y, z_, p)
        hand_on(1 - x, 1 - y, z_, p)

    @pl.loop(straight, PIECES)
    def _(p):
        copy(x, y, z, p, x_send, to_x).start()
        copy(x, y, z, p, y_send, to_y).start()

    @pl.loop(0, straight)
    def _(p):
        straight_on(z, p)

    @pl.loop(0, count + LATE)
    def _(i):
        now = jnp.minimum(i, count)
        later = jnp.minimum(i + 1, count)

        @pl.loop(now * slots // count, later * slots // count)
        def _(k):
            along(k, -1)
            along(k, 1)

            @pl.when(k == first // 2)
            def _():
                @pl.loop(0, 4 * TURNED)
                def _(j):
                    x_, y_, p = corner(j)

                    @pl.when(j // TURNED == 1)
                    def _():
                        from_x(z, p)

                    @pl.when(j // TURNED == 2)
                    def _():
                        from_y(z, p)

            @pl.when(k == first - TURNED)
            def _():
                @pl.loop(0, 4 * TURNED)
                def _(j):
                    x_, y_, p = corner(j)

                    @pl.when(j // TURNED == 3)
                    def _():
                        arrived(x_, y_, z, p)

                    along_z(x_, y_, z, p)
                    hand_on(x_, y_, z, p)

        @pl.when((i >= AHEAD) & (i < count + AHEAD))
        def _():
            from_plane(i - AHEAD)

        @pl.when(i >= LATE)
        def _():
            from_diagonal(i - LATE)

    def drain(sem, pieces):
        view = blocks_ref.at[0, 0, pl.ds(0, pieces * piece_rows)]
        pltpu.make_async_copy(view, view, sem).wait()

    over = (zs * straight + TURNED) * 3 // 2
    drain(x_send, over)
    drain(y_send, over)
    for at in range(zs):
        @pl.when(z == at)
        def _():
            if at < zs - 1:
                drain(up_send, (at + 1) * (straight + 4 * TURNED))
            if at > 0:
                drain(down_send, (zs - at) * (straight + 4 * TURNED))

    half = blocks_ref.at[0]
    pltpu.make_async_copy(half, half, core_send).wait()
    pltpu.make_async_copy(half, half, core_recv).wait()


def tile_kernel(all_variants, rows_ref, cols_ref, row_block, col_block, out_ref):
    t = pl.program_id(0)

    @pl.when(rows_ref[t] >= 0)
    def _():
        total = None
        for s in range(row_block.shape[1]):
            part = lax.dot_general(
                row_block[0, s, 0], col_block[0, s, 0], (((1,), (1,)), ((), ())),
                preferred_element_type=jnp.float32,
            )
            total = part if total is None else total + part
        out_ref[0] = total / all_variants

    @pl.when(rows_ref[t] < 0)
    def _():
        out_ref[...] = jnp.zeros_like(out_ref)


def tiles(all_variants, blocks, tile_rows, tile_cols):
    cores, slabs, _, rows, variants = blocks.shape
    count = tile_rows.shape[0]

    def place(t, rows_ref, cols_ref, which):
        block = jnp.maximum((rows_ref, cols_ref)[which][t], 0)
        return (lax.rem(block, cores), 0, block // cores, 0, 0)

    spec = lambda which: pl.BlockSpec(
        (1, slabs, 1, rows, variants), functools.partial(place, which=which)
    )
    return pl.pallas_call(
        functools.partial(tile_kernel, all_variants),
        out_shape=jax.ShapeDtypeStruct((count, rows, rows), jnp.float32),
        grid_spec=pltpu.PrefetchScalarGridSpec(
            num_scalar_prefetch=2,
            grid=(count,),
            in_specs=[spec(0), spec(1)],
            out_specs=pl.BlockSpec((1, rows, rows), lambda t, r, c: (t, 0, 0)),
        ),
        compiler_params=pltpu.CompilerParams(vmem_limit_bytes=32 * 1024 * 1024),
    )(tile_rows, tile_cols, blocks, blocks)


def fast(n, slabs, dosages, tile_rows, tile_cols):
    rows, variants = dosages.shape
    zs = n // 4
    dma = pltpu.SemaphoreType.DMA
    allele_freq, blocks = pl.pallas_call(
        functools.partial(gather_kernel, n),
        out_shape=(
            jax.ShapeDtypeStruct((1, variants), jnp.float32),
            jax.ShapeDtypeStruct((2, slabs, n // 2 * rows, variants), jnp.bfloat16),
        ),
        in_specs=[pl.BlockSpec(memory_space=pl.ANY)],
        out_specs=(pl.BlockSpec(memory_space=pltpu.VMEM), pl.BlockSpec(memory_space=pl.ANY)),
        scratch_shapes=[
            pltpu.VMEM((rows, variants), jnp.float32),
            pltpu.VMEM((n, 1, variants), jnp.float32),
            pltpu.VMEM((rows, variants), jnp.bfloat16),
            dma((n,)), dma((n,)), dma,
            dma, dma, dma, dma, dma,
            dma((2 * slabs, zs, PIECES)), dma,
        ],
        compiler_params=pltpu.CompilerParams(
            collective_id=0, has_side_effects=True, vmem_limit_bytes=60 * 1024 * 1024
        ),
    )(dosages)
    per_slab = tile_rows.shape[0] // slabs
    first = lax.axis_index("slab") * per_slab
    own_rows = lax.dynamic_slice_in_dim(tile_rows, first, per_slab, 0)
    own_cols = lax.dynamic_slice_in_dim(tile_cols, first, per_slab, 0)

    grm_tiles = tiles(variants * slabs, blocks.reshape(2, slabs, n // 2, rows, variants), own_rows, own_cols)
    return allele_freq.reshape(variants), grm_tiles


def general(n, slabs, dosages, tile_rows, tile_cols):
    rows, variants = dosages.shape
    allele_freq, spread = frequencies(lax.psum(jnp.sum(dosages, axis=0), "ind"), rows * n)
    standard = ((dosages - 2.0 * allele_freq) * lax.rsqrt(spread)).astype(jnp.bfloat16)
    groups = lax.all_gather(standard, "ind", axis=0)
    shares = tiles(variants * slabs, groups[None, None], tile_rows, tile_cols)
    return allele_freq, lax.psum_scatter(shares, "slab", scatter_dimension=0, tiled=True)


def solution(mesh):
    n, slabs = mesh.shape["ind"], mesh.shape["slab"]
    body = fast if slabs == 2 and n % 4 == 0 else general
    in_specs = (P("ind", "slab"), P("ind"), P("ind"))
    out_specs = (P("slab"), P(("ind", "slab"), None, None))
    return jax.shard_map(
        functools.partial(body, n, slabs),
        mesh=mesh, in_specs=in_specs, out_specs=out_specs, check_vma=False,
    )
```
